128 devices in a mesh: tile: 16 (over y_lo, z, core), member: 8 (over y_hi, x).
Axes of the slice: x: 4, y: 4 (y_hi: 2, y_lo: 2; y = y_hi * 2 + y_lo), z: 4, core: 2. Of those that a mesh axis runs over, the one named last changes fastest.
Arguments:
- coeffs: float32 [80, 32, 16384], P('member', None, 'tile'), may hold values from -6 to 6
- perturb: bfloat16 [2, 80, 32, 16384], P(None, 'member', None, 'tile'), may hold values from -1.25 to 1.25
- blocks: bfloat16 [16, 5, 1024, 1024], P('tile'), may hold values from -0.125 to 0.125
- neighbours: int32 [16, 5], P('tile'), may hold values from 0 to 15, as said below
- live: int32 [16], P('tile'), may hold values from 2 to 5, as said below
- obs_count: int32 [16], P('tile'), may hold values from 256 to 1024, as said below
- innovation: float32 [2, 32, 16384], P(None, None, 'tile'), may hold values from -6 to 6
- obs_weight: float32 [32, 16384], P(None, 'tile'), may hold values from 0.25 to 4
Outputs:
- increment: float32 [2, 32, 16384], P(None, None, ('tile', 'member'))
- gradient: float32 [80, 32, 16384], P('member', None, 'tile')
The draws below stay inside these ranges and needn't reach their ends.
Inputs may be any that keep to these rules, and one draw needn't show every extreme that they name: `neighbours`: each row lists 5 different tiles, each at a distance of at most 2 from the row's tile along the tile cycle (indices taken modulo 16); only the first live[i] slots of row i are used. Some tile has all 5 slots live. Observations of tile i lie in its first obs_count[i] columns.
All inputs are finite; a program needn't handle non-finite values.
Results may differ from the reference program's by a relative error of at most 0.0038.
Values may be sent and summed in bfloat16 or wider, within the bound.
A program may use at most 64 MiB of HBM per device.

```python
import math
import jax
import jax.numpy as jnp
from jax import lax

CELL_DEV = 1024
LEV = 32
TIMES = 2
REACH = 2
KMAX = 5
TILES = 16
CELLS = 16384
MEMBERS = 80


def draw_neighbours(key, part):
    key = jax.random.fold_in(key, 11)
    tile_keys = jax.random.split(key, TILES)
    offsets = jax.vmap(lambda single: jax.random.permutation(single, KMAX))(tile_keys) - REACH
    return ((jnp.arange(TILES)[:, None] + offsets) % TILES).astype(jnp.int32)


def draw_live(key, part):
    key = jax.random.fold_in(key, 12)
    first_key, second_key = jax.random.split(key)
    counts = jax.random.randint(first_key, (TILES,), 2, KMAX + 1)
    busiest = jax.random.randint(second_key, (), 0, TILES)
    return jnp.where(jnp.arange(TILES) == busiest, KMAX, counts).astype(jnp.int32)


def draw_obs_count(key, part):
    key = jax.random.fold_in(key, 13)
    first_key, second_key = jax.random.split(key)
    counts = jax.random.randint(first_key, (TILES,), CELL_DEV // 4, CELL_DEV + 1)
    fullest = jax.random.randint(second_key, (), 0, TILES)
    tile_ids = jnp.arange(TILES)
    counts = jnp.where(tile_ids == fullest, CELL_DEV, counts)
    counts = jnp.where(tile_ids == (fullest + 1) % TILES, CELL_DEV // 4, counts)
    return counts.astype(jnp.int32)


def levels(own_key, shape, shards, smallest, high):
    def one(position, blocks):
        draws = jax.random.uniform(jax.random.fold_in(jax.random.fold_in(own_key, 6), position), (blocks,), jnp.float32, smallest / len(shards), high / len(shards))
        return jnp.repeat(jnp.exp(draws), shape[position] // blocks).reshape((-1,) + (1,) * (len(shape) - position - 1))

    loudness = one(*shards[0])
    for cut in shards[1:]:
        loudness = loudness * one(*cut)
    return loudness


def noise(own_key, extent, spread, reach, cuts=(), held_as=jnp.bfloat16):
    drawn = jax.random.normal(own_key, extent, jnp.float32) * spread
    if len(cuts) > 0:
        drawn = levels(own_key, extent, cuts, -0.22, 0.18) * drawn
    return jnp.clip(drawn, min=-reach, max=reach).astype(held_as)


def setup_inputs(seed: int = 0) -> dict:
    key_list = jax.random.split(jax.random.key(seed), 9)
    coeffs = noise(key_list[0], (MEMBERS, LEV, CELLS), 1.0, 6.0, ((0, 8), (2, 16)), jnp.float32)
    perturb = noise(key_list[1], (TIMES, MEMBERS, LEV, CELLS), (MEMBERS // 4) ** -0.5, 1.25, ((1, 8), (3, 16)))
    blocks = noise(key_list[2], (TILES, KMAX, CELL_DEV, CELL_DEV), (CELL_DEV * 2) ** -0.5, 0.125, ((0, 16),))
    neighbours = draw_neighbours(jax.random.fold_in(key_list[8], 71), 0)
    live = draw_live(jax.random.fold_in(key_list[8], 71), 0)
    obs_count = draw_obs_count(jax.random.fold_in(key_list[8], 71), 0)
    innovation = noise(key_list[6], (TIMES, LEV, CELLS), 1.0, 6.0, ((2, 16),), jnp.float32)
    obs_weight = jnp.clip(jnp.exp(math.log(4.0) - 2.7725887 * jax.random.uniform(key_list[7], (LEV, CELLS), jnp.float32) ** levels(key_list[7], (LEV, CELLS), ((1, 16),), -0.2, 0.2)), 0.25, 4.0)
    return dict(coeffs=coeffs, perturb=perturb, blocks=blocks, neighbours=neighbours, live=live, obs_count=obs_count, innovation=innovation, obs_weight=obs_weight)


def reference(coeffs, perturb, blocks, neighbours, live, obs_count, innovation, obs_weight):
    row_count = MEMBERS * LEV
    coeff_half = coeffs.astype(jnp.bfloat16).reshape(row_count, TILES, CELL_DEV)
    slot_ids = jnp.arange(KMAX)

    def forward(tile_id):
        sources = neighbours[tile_id]
        slot_live = slot_ids < live[tile_id]
        pieces = jnp.take(coeff_half, sources, axis=1).astype(jnp.float32)
        product = jnp.einsum('rkc,kcd->rkd', pieces, blocks[tile_id].astype(jnp.float32))
        return jnp.sum(jnp.where(slot_live[None, :, None], product, 0.0), axis=1)

    localized = lax.map(forward, jnp.arange(TILES))
    localized = jnp.transpose(localized, (1, 0, 2)).reshape(MEMBERS, LEV, CELLS)
    increment = jnp.sum(perturb.astype(jnp.float32) * localized[None], axis=1)
    column_ids = jnp.arange(CELLS)
    observed = (column_ids % CELL_DEV) < obs_count[column_ids // CELL_DEV]
    residual = obs_weight[None] * jnp.where(observed[None, None, :], increment - innovation, 0.0)
    adjoint_in = jnp.sum(perturb.astype(jnp.float32) * residual[:, None], axis=0)
    adjoint_in = adjoint_in.astype(jnp.bfloat16).reshape(row_count, TILES, CELL_DEV)
    tile_ids = jnp.arange(TILES)

    def backward(accum, tile_id):
        sources = neighbours[tile_id]
        slot_live = slot_ids < live[tile_id]
        local_in = lax.dynamic_index_in_dim(adjoint_in, tile_id, 1, keepdims=False).astype(jnp.float32)
        product = jnp.einsum('rd,kcd->krc', local_in, blocks[tile_id].astype(jnp.float32))
        one_hot = ((sources[:, None] == tile_ids[None, :]) & slot_live[:, None]).astype(jnp.float32)
        return accum + jnp.einsum('kt,krc->rtc', one_hot, product), None

    adjoint, unused = lax.scan(backward, jnp.zeros((row_count, TILES, CELL_DEV), jnp.float32), tile_ids)
    gradient = coeffs + adjoint.reshape(MEMBERS, LEV, CELLS)
    return increment, gradient
```

```python
import functools

import jax
import jax.numpy as jnp
from jax import lax
from jax.experimental import pallas as pl
from jax.experimental.pallas import tpu as pltpu
from jax.sharding import PartitionSpec as P

MESH = pl.DeviceIdType.MESH
F32, BF16 = jnp.float32, jnp.bfloat16
CHUNKS = (8, 8, 8, 8)
COLS = 256


def kernel(tiles, groups, coeffs, perturb, blocks, neighbours, live, count, innovation, weight,
           inc_out, adj_out,
           coeff_v, pert_v, pert_f, block_v, block_t, innov_v, weight_v,
           half, zrecv, precv, loc, part, psend, mrecv, total, ain,
           csend, crecv, bsend, brecv, acc,
           load_sem, z_s, z_r, o_s, o_r, f_s, f_r, m_s, m_r, c_s, c_r, b_s, b_r):
    members, levels, width = coeffs.shape
    slots = blocks.shape[1]
    tile, group = lax.axis_index("tile"), lax.axis_index("member")
    side = 1 - 2 * lax.rem(tile, 2)

    def at(step):
        return {"tile": lax.rem(tile + step * side + tiles, tiles)}

    partner, ahead, behind = at(1), at(2), at(-2)
    peers = [{"member": lax.rem(group + d, groups)} for d in range(1, groups)]

    def remote(src, dst, send, recv, device):
        return pltpu.make_async_remote_copy(
            src_ref=src, dst_ref=dst, send_sem=send, recv_sem=recv,
            device_id=device, device_id_type=MESH)

    loads = [
        pltpu.make_async_copy(coeffs, coeff_v, load_sem.at[0]),
        pltpu.make_async_copy(perturb, pert_v, load_sem.at[1]),
        pltpu.make_async_copy(innovation, innov_v, load_sem.at[2]),
        pltpu.make_async_copy(weight, weight_v, load_sem.at[3]),
    ]
    for k in range(slots):
        loads.append(pltpu.make_async_copy(blocks.at[0, k], block_v.at[k], load_sem.at[4 + k]))
    loads[0].start()
    barrier = pltpu.get_barrier_semaphore()
    for device in [ahead, behind, partner] + peers:
        pl.semaphore_signal(barrier, inc=1, device_id=device, device_id_type=MESH)
    for load in loads[1:]:
        load.start()

    slot_at, live_at = {}, {}
    for step in range(-2, 3):
        slot, alive = jnp.int32(0), jnp.int32(0)
        for k in range(slots):
            hit = lax.rem((neighbours[0, k] - tile) * side + 2 * tiles - step, tiles) == 0
            slot = jnp.where(hit, k, slot)
            alive = jnp.where(hit, jnp.where(k < live[0], 1, 0), alive)
        slot_at[step], live_at[step] = slot, alive

    starts = [sum(CHUNKS[:c]) for c in range(len(CHUNKS))]

    def rows(c):
        return pl.ds(members * starts[c], members * CHUNKS[c])

    loads[0].wait()
    for c, size in enumerate(CHUNKS):
        lo = starts[c]
        for m in range(0, members, 2):
            two = coeff_v[m:m + 2, lo:lo + size, :].reshape(2 * size, width)
            half[pl.ds(members * lo + m * size, 2 * size)] = two.astype(BF16)

    pl.semaphore_wait(barrier, 3 + len(peers))

    pending = []

    def start(copy):
        copy.start()
        pending.append(copy)
        return copy

    zcopies, ocopies = [], []
    for c in range(len(CHUNKS)):
        r = rows(c)
        zcopies.append((
            start(remote(half.at[r], zrecv.at[0, r], z_s.at[0, c], z_r.at[0, c], behind)),
            start(remote(half.at[r], zrecv.at[1, r], z_s.at[1, c], z_r.at[1, c], ahead))))
        ocopies.append(start(remote(half.at[r], precv.at[0, r], o_s.at[c], o_r.at[c], partner)))

    def forward(piece, r, step, first=False):
        value = piece[...]
        for n in range(0, width, COLS):
            product = jnp.dot(value, block_v[slot_at[step], :, n:n + COLS], preferred_element_type=F32)
            product = jnp.where(live_at[step] > 0, product, 0.0)
            loc[r, n:n + COLS] = product if first else loc[r, n:n + COLS] + product

    loads[1].wait()
    for t in range(2):
        for m in range(members):
            pert_f[t, m] = pert_v[t, m].astype(F32)
    for load in loads[4:]:
        load.wait()
    everything = pl.ds(0, members * levels)
    forward(half, everything, 0, first=True)
    for k in range(slots):
        for n in range(0, width, COLS):
            block_t[k, :, n:n + COLS] = block_v[k, n:n + COLS, :].T
    for copy in ocopies:
        copy.wait_recv()
    forward(precv.at[0], everything, 1)
    loads[2].wait()
    loads[3].wait()

    mcopies = {}

    def contract(c):
        r, lo, size = rows(c), starts[c], CHUNKS[c]
        near, far = zcopies[c]
        near.wait_recv()
        passed = start(remote(zrecv.at[0, r], precv.at[1, r], f_s.at[c], f_r.at[c], partner))
        forward(zrecv.at[0, r], r, 2)
        far.wait_recv()
        forward(zrecv.at[1, r], r, -2)
        passed.wait_recv()
        forward(precv.at[1, r], r, -1)
        for t in range(2):
            value = jnp.zeros((size, width), F32)
            for m in range(members):
                value = value + pert_f[t, m, lo:lo + size, :] * loc[pl.ds(members * lo + m * size, size)]
            part[t, lo:lo + size, :] = value
        both = part[:, lo:lo + size, :].reshape(2 * size, width)
        mine = pl.ds(2 * lo, 2 * size)
        psend[mine] = both.astype(BF16)
        mcopies[c] = [
            start(remote(psend.at[mine], mrecv.at[d, mine], m_s.at[d, c], m_r.at[d, c], peers[d]))
            for d in range(len(peers))]

    column = lax.broadcasted_iota(jnp.int32, (1, 1, width), 2)
    observed = column < count[0]
    bcopies, kept = {}, {}

    def product(value, step, n):
        out = jnp.dot(value, block_t[slot_at[step], :, n:n + COLS], preferred_element_type=F32)
        return jnp.where(live_at[step] > 0, out, 0.0)

    def adjoint(c):
        r, lo, size = rows(c), starts[c], CHUNKS[c]
        mine = pl.ds(2 * lo, 2 * size)
        for copy in mcopies[c]:
            copy.wait_recv()
        summed = part[:, lo:lo + size, :]
        for d in range(len(peers)):
            summed = summed + mrecv[d, mine].astype(F32).reshape(2, size, width)
        total[:, lo:lo + size, :] = summed
        residual = weight_v[lo:lo + size, :][None] * jnp.where(
            observed, summed - innov_v[:, lo:lo + size, :], 0.0)
        for m in range(0, members, 2):
            two = pert_f[0, m:m + 2, lo:lo + size, :] * residual[0][None]
            two = two + pert_f[1, m:m + 2, lo:lo + size, :] * residual[1][None]
            ain[pl.ds(members * lo + m * size, 2 * size)] = two.reshape(2 * size, width).astype(BF16)
        value = ain[r]
        for n in range(0, width, COLS):
            csend[0, r, n:n + COLS] = product(value, -1, n).astype(BF16)
        shared = start(remote(csend.at[0, r], crecv.at[0, r], c_s.at[0, c], c_r.at[0, c], partner))
        for n in range(0, width, COLS):
            bsend[0, r, n:n + COLS] = product(value, -2, n).astype(BF16)
        lone = start(remote(bsend.at[0, r], brecv.at[0, r], b_s.at[0, c], b_r.at[0, c], behind))
        for n in range(0, width, COLS):
            acc[r, n:n + COLS] = product(value, 2, n)
        shared.wait_recv()
        bsend[1, r] = (acc[r] + crecv[0, r].astype(F32)).astype(BF16)
        pair = start(remote(bsend.at[1, r], brecv.at[1, r], b_s.at[1, c], b_r.at[1, c], ahead))
        for n in range(0, width, COLS):
            csend[1, r, n:n + COLS] = product(value, 1, n).astype(BF16)
        given = start(remote(csend.at[1, r], crecv.at[1, r], c_s.at[1, c], c_r.at[1, c], partner))
        for n in range(0, width, COLS):
            acc[r, n:n + COLS] = product(value, 0, n)
        bcopies[c] = (given, lone, pair)

    def finish(c):
        lo, size = starts[c], CHUNKS[c]
        for copy in bcopies[c]:
            copy.wait_recv()
        for m in range(0, members, 2):
            r = pl.ds(members * lo + m * size, 2 * size)
            value = acc[r] + crecv[1, r].astype(F32)
            value = value + (brecv[0, r].astype(F32) + brecv[1, r].astype(F32))
            adj_out[m:m + 2, lo:lo + size, :] = value.reshape(2, size, width)

    order = [("c", 0), ("c", 1), ("c", 2), ("a", 0), ("c", 3), ("a", 1), ("a", 2), ("a", 3)]
    for kind, c in order:
        (contract if kind == "c" else adjoint)(c)
    own = pl.multiple_of(group * (width // groups), width // groups)
    inc_out[...] = total[:, :, pl.ds(own, width // groups)]
    for c in range(len(CHUNKS)):
        finish(c)
    for copy in pending:
        copy.wait_send()


def shards(coeffs, perturb, blocks, neighbours, live, obs_count, innovation, obs_weight):
    members, levels, width = coeffs.shape
    slots = blocks.shape[1]
    tiles, groups = lax.axis_size("tile"), lax.axis_size("member")
    row_count, chunks, peers = members * levels, len(CHUNKS), groups - 1
    anywhere = pl.BlockSpec(memory_space=pl.ANY)
    scalars = pl.BlockSpec(memory_space=pltpu.SMEM)
    vmem = pl.BlockSpec(memory_space=pltpu.VMEM)
    dma = pltpu.SemaphoreType.DMA
    increment, adjoint = pl.pallas_call(
        functools.partial(kernel, tiles, groups),
        out_shape=(
            jax.ShapeDtypeStruct((2, levels, width // groups), F32),
            jax.ShapeDtypeStruct((members, levels, width), F32),
        ),
        in_specs=[anywhere, anywhere, anywhere, scalars, scalars, scalars, anywhere, anywhere],
        out_specs=(vmem, vmem),
        scratch_shapes=[
            pltpu.VMEM((members, levels, width), F32),
            pltpu.VMEM((2, members, levels, width), BF16),
            pltpu.VMEM((2, members, levels, width), F32),
            pltpu.VMEM((slots, width, width), BF16),
            pltpu.VMEM((slots, width, width), BF16),
            pltpu.VMEM((2, levels, width), F32),
            pltpu.VMEM((levels, width), F32),
            pltpu.VMEM((row_count, width), BF16),
            pltpu.VMEM((2, row_count, width), BF16),
            pltpu.VMEM((2, row_count, width), BF16),
            pltpu.VMEM((row_count, width), F32),
            pltpu.VMEM((2, levels, width), F32),
            pltpu.VMEM((2 * levels, width), BF16),
            pltpu.VMEM((peers, 2 * levels, width), BF16),
            pltpu.VMEM((2, levels, width), F32),
            pltpu.VMEM((row_count, width), BF16),
            pltpu.VMEM((2, row_count, width), BF16),
            pltpu.VMEM((2, row_count, width), BF16),
            pltpu.VMEM((2, row_count, width), BF16),
            pltpu.VMEM((2, row_count, width), BF16),
            pltpu.VMEM((row_count, width), F32),
            dma((4 + slots,)),
            dma((2, chunks)), dma((2, chunks)),
            dma((chunks,)), dma((chunks,)),
            dma((chunks,)), dma((chunks,)),
            dma((peers, chunks)), dma((peers, chunks)),
            dma((2, chunks)), dma((2, chunks)),
            dma((2, chunks)), dma((2, chunks)),
        ],
        compiler_params=pltpu.CompilerParams(
            collective_id=0, has_side_effects=True, vmem_limit_bytes=56 * 1024 * 1024),
        cost_estimate=pl.CostEstimate(
            flops=4 * row_count * width * width * slots, bytes_accessed=16 * 1024 * 1024, transcendentals=0),
    )(coeffs, perturb, blocks, neighbours, live, obs_count, innovation, obs_weight)
    return increment, coeffs + adjoint


def solution(mesh):
    placed = (
        P("member", None, "tile"),
        P(None, "member", None, "tile"),
        P("tile", None, None, None),
        P("tile", None),
        P("tile"),
        P("tile"),
        P(None, None, "tile"),
        P(None, "tile"),
    )
    return jax.shard_map(
        shards,
        mesh=mesh,
        in_specs=placed,
        out_specs=(P(None, None, ("tile", "member")), P("member", None, "tile")),
        check_vma=False,
    )
```

```python
import functools

import jax
import jax.numpy as jnp
from jax import lax
from jax.experimental import pallas as pl
from jax.experimental.pallas import tpu as pltpu
from jax.sharding import PartitionSpec as P

MESH = pl.DeviceIdType.MESH
F32, BF16 = jnp.float32, jnp.bfloat16
CHUNKS = (8, 8, 8, 8)
X_FIRST = (0, 1)
ORDER = (
    "z0", "t0", "x0", "z1", "t1", "x1", "z2", "t2", "m0", "x2", "z3", "t3",
    "m1", "x3", "t4", "m2", "a0", "m3", "a1", "a2", "a3",
)
COLS = 256


def kernel(tiles, groups, coeffs, perturb, blocks, neighbours_in, live_in, count_in, innovation, weight,
           inc_out, grad_out,
           coeff_v, pert_v, pert_f, block_v, block_t, innov_v, weight_v,
           half, zrecv, precv, loc, part, psend, xrecv, ysend, yrecv, total, ain,
           csend, crecv, bsend, brecv, acc,
           neighbours, live, count, scalar_sem,
           load_sem, z_s, z_r, o_s, o_r, f_s, f_r, m_s, m_r, g_s, g_r, c_s, c_r, b_s, b_r):
    members, levels, width = coeffs.shape
    slots = blocks.shape[1]
    tile, group = lax.axis_index("tile"), lax.axis_index("member")
    side = 1 - 2 * lax.rem(tile, 2)

    def at(step):
        return {"tile": lax.rem(tile + step * side + tiles, tiles)}

    partner, ahead, behind = at(1), at(2), at(-2)
    line = groups // 2
    place = lax.rem(group, line)
    peers = [{"member": group - place + lax.rem(place + d, line)} for d in range(1, line)]
    across = {"member": lax.rem(group + line, groups)}

    def remote(src, dst, send, recv, device):
        return pltpu.make_async_remote_copy(
            src_ref=src, dst_ref=dst, send_sem=send, recv_sem=recv,
            device_id=device, device_id_type=MESH)

    first = [pltpu.make_async_copy(coeffs.at[m], coeff_v.at[m], load_sem.at[4 + slots + m]) for m in range(members)]
    scalars = [
        pltpu.make_async_copy(neighbours_in, neighbours, scalar_sem.at[0]),
        pltpu.make_async_copy(live_in, live, scalar_sem.at[1]),
        pltpu.make_async_copy(count_in, count, scalar_sem.at[2]),
    ]
    loads = [
        pltpu.make_async_copy(perturb.at[0], pert_v.at[0], load_sem.at[0]),
        pltpu.make_async_copy(perturb.at[1], pert_v.at[1], load_sem.at[1]),
        pltpu.make_async_copy(innovation, innov_v, load_sem.at[2]),
        pltpu.make_async_copy(weight, weight_v, load_sem.at[3]),
    ]
    for k in range(slots):
        loads.append(pltpu.make_async_copy(blocks.at[0, k], block_v.at[k], load_sem.at[4 + k]))
    barrier = pltpu.get_barrier_semaphore()
    for device in [ahead, behind, partner, across] + peers:
        pl.semaphore_signal(barrier, inc=1, device_id=device, device_id_type=MESH)
    for load in first + scalars:
        load.start()

    starts = [sum(CHUNKS[:c]) for c in range(len(CHUNKS))]

    def rows(c):
        return pl.ds(members * starts[c], members * CHUNKS[c])

    for load in first:
        load.wait()
    for c, size in enumerate(CHUNKS):
        lo = starts[c]
        for m in range(0, members, 2):
            two = coeff_v[m:m + 2, lo:lo + size, :].reshape(2 * size, width)
            half[pl.ds(members * lo + m * size, 2 * size)] = two.astype(BF16)

    pl.semaphore_wait(barrier, 4 + len(peers))

    pending = []

    def start(copy):
        copy.start()
        pending.append(copy)
        return copy

    zcopies, ocopies = [], []
    for c in range(len(CHUNKS)):
        r = rows(c)
        zcopies.append((
            start(remote(half.at[r], zrecv.at[0, r], z_s.at[0, c], z_r.at[0, c], behind)),
            start(remote(half.at[r], zrecv.at[1, r], z_s.at[1, c], z_r.at[1, c], ahead))))
        if c == 0:
            for load in loads:
                load.start()
        ocopies.append(start(remote(half.at[r], precv.at[0, r], o_s.at[c], o_r.at[c], partner)))

    for load in scalars:
        load.wait()
    slot_at, live_at = {}, {}
    for step in range(-2, 3):
        slot, alive = jnp.int32(0), jnp.int32(0)
        for k in range(slots):
            hit = lax.rem((neighbours[0, k] - tile) * side + 2 * tiles - step, tiles) == 0
            slot = jnp.where(hit, k, slot)
            alive = jnp.where(hit, jnp.where(k < live[0], 1, 0), alive)
        slot_at[step], live_at[step] = slot, alive

    def forward(piece, r, step, first=False):
        value = piece[...]
        for n in range(0, width, COLS):
            product = jnp.dot(value, block_v[slot_at[step], :, n:n + COLS], preferred_element_type=F32)
            product = jnp.where(live_at[step] > 0, product, 0.0)
            loc[r, n:n + COLS] = product if first else loc[r, n:n + COLS] + product

    loads[0].wait()
    loads[1].wait()
    for t in range(2):
        for m in range(members):
            pert_f[t, m] = pert_v[t, m].astype(F32)
    for load in loads[4:]:
        load.wait()
    everything = pl.ds(0, members * levels)
    forward(half, everything, 0, first=True)

    def turn(k):
        for n in range(0, width, COLS):
            block_t[k, :, n:n + COLS] = block_v[k, n:n + COLS, :].T

    for copy in ocopies:
        copy.wait_recv()
    forward(precv.at[0], everything, 1)
    loads[2].wait()
    loads[3].wait()

    xcopies, ycopies, passing = {}, {}, {}

    def arrive(c):
        r = rows(c)
        near, far = zcopies[c]
        near.wait_recv()
        passing[c] = start(remote(zrecv.at[0, r], precv.at[1, r], f_s.at[c], f_r.at[c], partner))
        forward(zrecv.at[0, r], r, 2)
        far.wait_recv()
        forward(zrecv.at[1, r], r, -2)

    def contract(c):
        r, lo, size = rows(c), starts[c], CHUNKS[c]
        passing[c].wait_recv()
        forward(precv.at[1, r], r, -1)
        for t in range(2):
            value = jnp.zeros((size, width), F32)
            for m in range(members):
                value = value + pert_f[t, m, lo:lo + size, :] * loc[pl.ds(members * lo + m * size, size)]
            part[t, lo:lo + size, :] = value
        both = part[:, lo:lo + size, :].reshape(2 * size, width)
        mine = pl.ds(2 * lo, 2 * size)
        psend[mine] = both.astype(BF16)
        (along if c in X_FIRST else beyond)(c, psend)

    def along(c, source):
        mine = pl.ds(2 * starts[c], 2 * CHUNKS[c])
        xcopies[c] = [
            start(remote(source.at[mine], xrecv.at[d, mine], m_s.at[d, c], m_r.at[d, c], peers[d]))
            for d in range(len(peers))]

    def beyond(c, source):
        mine = pl.ds(2 * starts[c], 2 * CHUNKS[c])
        ycopies[c] = start(remote(source.at[mine], yrecv.at[mine], g_s.at[c], g_r.at[c], across))

    def with_line(c, summed):
        mine = pl.ds(2 * starts[c], 2 * CHUNKS[c])
        for copy in xcopies[c]:
            copy.wait_recv()
        for d in range(len(peers)):
            summed = summed + xrecv[d, mine].astype(F32)
        return summed

    def with_across(c, summed):
        ycopies[c].wait_recv()
        return summed + yrecv[pl.ds(2 * starts[c], 2 * CHUNKS[c])].astype(F32)

    def merge(c):
        lo, size = starts[c], CHUNKS[c]
        mine = pl.ds(2 * lo, 2 * size)
        summed = part[:, lo:lo + size, :].reshape(2 * size, width)
        summed = (with_line if c in X_FIRST else with_across)(c, summed)
        part[:, lo:lo + size, :] = summed.reshape(2, size, width)
        ysend[mine] = summed.astype(BF16)
        (beyond if c in X_FIRST else along)(c, ysend)

    column = lax.broadcasted_iota(jnp.int32, (1, 1, width), 2)
    observed = column < count[0]
    bcopies, kept = {}, {}

    def product(value, step, n):
        out = jnp.dot(value, block_t[slot_at[step], :, n:n + COLS], preferred_element_type=F32)
        return jnp.where(live_at[step] > 0, out, 0.0)

    def adjoint(c):
        r, lo, size = rows(c), starts[c], CHUNKS[c]
        summed = part[:, lo:lo + size, :].reshape(2 * size, width)
        summed = (with_across if c in X_FIRST else with_line)(c, summed).reshape(2, size, width)
        total[:, lo:lo + size, :] = summed
        residual = weight_v[lo:lo + size, :][None] * jnp.where(
            observed, summed - innov_v[:, lo:lo + size, :], 0.0)
        for m in range(0, members, 2):
            two = pert_f[0, m:m + 2, lo:lo + size, :] * residual[0][None]
            two = two + pert_f[1, m:m + 2, lo:lo + size, :] * residual[1][None]
            ain[pl.ds(members * lo + m * size, 2 * size)] = two.reshape(2 * size, width).astype(BF16)
        value = ain[r]
        for n in range(0, width, COLS):
            csend[0, r, n:n + COLS] = product(value, -1, n).astype(BF16)
        shared = start(remote(csend.at[0, r], crecv.at[0, r], c_s.at[0, c], c_r.at[0, c], partner))
        for n in range(0, width, COLS):
            bsend[0, r, n:n + COLS] = product(value, -2, n).astype(BF16)
        lone = start(remote(bsend.at[0, r], brecv.at[0, r], b_s.at[0, c], b_r.at[0, c], behind))
        for n in range(0, width, COLS):
            acc[r, n:n + COLS] = product(value, 2, n)
        shared.wait_recv()
        bsend[1, r] = (acc[r] + crecv[0, r].astype(F32)).astype(BF16)
        pair = start(remote(bsend.at[1, r], brecv.at[1, r], b_s.at[1, c], b_r.at[1, c], ahead))
        for n in range(0, width, COLS):
            csend[1, r, n:n + COLS] = product(value, 1, n).astype(BF16)
        given = start(remote(csend.at[1, r], crecv.at[1, r], c_s.at[1, c], c_r.at[1, c], partner))
        for n in range(0, width, COLS):
            acc[r, n:n + COLS] = product(value, 0, n)
        bcopies[c] = (given, lone, pair)

    def finish(c):
        lo, size = starts[c], CHUNKS[c]
        for copy in bcopies[c]:
            copy.wait_recv()
        for m in range(0, members, 2):
            r = pl.ds(members * lo + m * size, 2 * size)
            value = acc[r] + crecv[1, r].astype(F32)
            value = value + coeff_v[m:m + 2, lo:lo + size, :].reshape(2 * size, width)
            value = value + (brecv[0, r].astype(F32) + brecv[1, r].astype(F32))
            grad_out[m:m + 2, lo:lo + size, :] = value.reshape(2, size, width)

    steps = {"z": arrive, "x": contract, "m": merge, "a": adjoint, "t": turn}
    for step in ORDER:
        steps[step[0]](int(step[1:]))
    own = pl.multiple_of(group * (width // groups), width // groups)
    inc_out[...] = total[:, :, pl.ds(own, width // groups)]
    for c in range(len(CHUNKS)):
        finish(c)
    for copy in pending:
        copy.wait_send()


def shards(coeffs, perturb, blocks, neighbours, live, obs_count, innovation, obs_weight):
    members, levels, width = coeffs.shape
    slots = blocks.shape[1]
    tiles, groups = lax.axis_size("tile"), lax.axis_size("member")
    row_count, chunks, peers = members * levels, len(CHUNKS), groups // 2 - 1
    anywhere = pl.BlockSpec(memory_space=pl.ANY)
    vmem = pl.BlockSpec(memory_space=pltpu.VMEM)
    dma = pltpu.SemaphoreType.DMA
    held = pl.pallas_call(
        functools.partial(kernel, tiles, groups),
        out_shape=(
            pltpu.VMEM((2, levels, width // groups), F32),
            pltpu.VMEM((members, levels, width), F32),
        ),
        in_specs=[anywhere] * 8,
        out_specs=(vmem, vmem),
        scratch_shapes=[
            pltpu.VMEM((members, levels, width), F32),
            pltpu.VMEM((2, members, levels, width), BF16),
            pltpu.VMEM((2, members, levels, width), F32),
            pltpu.VMEM((slots, width, width), BF16),
            pltpu.VMEM((slots, width, width), BF16),
            pltpu.VMEM((2, levels, width), F32),
            pltpu.VMEM((levels, width), F32),
            pltpu.VMEM((row_count, width), BF16),
            pltpu.VMEM((2, row_count, width), BF16),
            pltpu.VMEM((2, row_count, width), BF16),
            pltpu.VMEM((row_count, width), F32),
            pltpu.VMEM((2, levels, width), F32),
            pltpu.VMEM((2 * levels, width), BF16),
            pltpu.VMEM((peers, 2 * levels, width), BF16),
            pltpu.VMEM((2 * levels, width), BF16),
            pltpu.VMEM((2 * levels, width), BF16),
            pltpu.VMEM((2, levels, width), F32),
            pltpu.VMEM((row_count, width), BF16),
            pltpu.VMEM((2, row_count, width), BF16),
            pltpu.VMEM((2, row_count, width), BF16),
            pltpu.VMEM((2, row_count, width), BF16),
            pltpu.VMEM((2, row_count, width), BF16),
            pltpu.VMEM((row_count, width), F32),
            pltpu.SMEM((1, slots), jnp.int32),
            pltpu.SMEM((1,), jnp.int32),
            pltpu.SMEM((1,), jnp.int32),
            dma((3,)),
            dma((members + 4 + slots,)),
            dma((2, chunks)), dma((2, chunks)),
            dma((chunks,)), dma((chunks,)),
            dma((chunks,)), dma((chunks,)),
            dma((peers, chunks)), dma((peers, chunks)),
            dma((chunks,)), dma((chunks,)),
            dma((2, chunks)), dma((2, chunks)),
            dma((2, chunks)), dma((2, chunks)),
        ],
        compiler_params=pltpu.CompilerParams(
            collective_id=0, has_side_effects=True, vmem_limit_bytes=56 * 1024 * 1024),
        cost_estimate=pl.CostEstimate(
            flops=4 * row_count * width * width * slots, bytes_accessed=16 * 1024 * 1024, transcendentals=0),
    )(coeffs, perturb, blocks, neighbours, live, obs_count, innovation, obs_weight)
    return held


def solution(mesh):
    placed = (
        P("member", None, "tile"),
        P(None, "member", None, "tile"),
        P("tile", None, None, None),
        P("tile", None),
        P("tile"),
        P("tile"),
        P(None, None, "tile"),
        P(None, "tile"),
    )
    return jax.shard_map(
        shards,
        mesh=mesh,
        in_specs=placed,
        out_specs=(P(None, None, ("tile", "member")), P("member", None, "tile")),
        check_vma=False,
    )
```

```python
import functools

import jax
import jax.numpy as jnp
from jax import lax
from jax.experimental import pallas as pl
from jax.experimental.pallas import tpu as pltpu
from jax.sharding import PartitionSpec as P

MESH = pl.DeviceIdType.MESH
F32, BF16 = jnp.float32, jnp.bfloat16
CHUNKS = (8, 8, 8, 8)
X_FIRST = (0, 1)
ORDER = (
    "z0", "t0", "x0", "t1", "z1", "t2", "x1", "t3", "z2", "m0", "x2", "t4", "z3", "x3",
    "m1", "a0", "m2", "b0", "m3", "a1", "b1", "a2", "b2", "a3", "b3",
)
COLS = 256


def kernel(tiles, groups, coeffs, perturb, blocks, neighbours_in, live_in, count_in, innovation, weight,
           inc_out, grad_out,
           coeff_v, pert_v, pert_f, block_v, block_t, innov_v, weight_v,
           half, zrecv, precv, loc, part, psend, xrecv, ysend, yrecv, total, ain,
           csend, crecv, bsend, brecv, acc,
           neighbours, live, count, scalar_sem,
           load_sem, z_s, z_r, o_s, o_r, f_s, f_r, m_s, m_r, g_s, g_r, c_s, c_r, b_s, b_r):
    members, levels, width = coeffs.shape
    slots = blocks.shape[1]
    tile, group = lax.axis_index("tile"), lax.axis_index("member")
    side = 1 - 2 * lax.rem(tile, 2)

    def at(step):
        return {"tile": lax.rem(tile + step * side + tiles, tiles)}

    partner, ahead, behind = at(1), at(2), at(-2)
    line = groups // 2
    place = lax.rem(group, line)
    peers = [{"member": group - place + lax.rem(place + d, line)} for d in range(1, line)]
    across = {"member": lax.rem(group + line, groups)}

    def remote(src, dst, send, recv, device):
        return pltpu.make_async_remote_copy(
            src_ref=src, dst_ref=dst, send_sem=send, recv_sem=recv,
            device_id=device, device_id_type=MESH)

    first = [pltpu.make_async_copy(coeffs.at[m], coeff_v.at[m], load_sem.at[4 + slots + m]) for m in range(members)]
    scalars = [
        pltpu.make_async_copy(neighbours_in, neighbours, scalar_sem.at[0]),
        pltpu.make_async_copy(live_in, live, scalar_sem.at[1]),
        pltpu.make_async_copy(count_in, count, scalar_sem.at[2]),
    ]
    loads = [
        pltpu.make_async_copy(perturb.at[0], pert_v.at[0], load_sem.at[0]),
        pltpu.make_async_copy(perturb.at[1], pert_v.at[1], load_sem.at[1]),
        pltpu.make_async_copy(innovation, innov_v, load_sem.at[2]),
        pltpu.make_async_copy(weight, weight_v, load_sem.at[3]),
    ]
    for k in range(slots):
        loads.append(pltpu.make_async_copy(blocks.at[0, k], block_v.at[k], load_sem.at[4 + k]))
    barrier = pltpu.get_barrier_semaphore()
    for device in [ahead, behind, partner, across] + peers:
        pl.semaphore_signal(barrier, inc=1, device_id=device, device_id_type=MESH)
    for load in first + scalars:
        load.start()

    starts = [sum(CHUNKS[:c]) for c in range(len(CHUNKS))]

    def rows(c):
        return pl.ds(members * starts[c], members * CHUNKS[c])

    for load in first:
        load.wait()
    for c, size in enumerate(CHUNKS):
        lo = starts[c]
        for m in range(0, members, 2):
            two = coeff_v[m:m + 2, lo:lo + size, :].reshape(2 * size, width)
            half[pl.ds(members * lo + m * size, 2 * size)] = two.astype(BF16)

    pl.semaphore_wait(barrier, 4 + len(peers))

    pending = []

    def start(copy):
        copy.start()
        pending.append(copy)
        return copy

    zcopies, ocopies = [], []
    for c in range(len(CHUNKS)):
        r = rows(c)
        zcopies.append((
            start(remote(half.at[r], zrecv.at[0, r], z_s.at[0, c], z_r.at[0, c], behind)),
            start(remote(half.at[r], zrecv.at[1, r], z_s.at[1, c], z_r.at[1, c], ahead))))
        if c == 0:
            for load in loads:
                load.start()
        ocopies.append(start(remote(half.at[r], precv.at[0, r], o_s.at[c], o_r.at[c], partner)))

    for load in scalars:
        load.wait()
    slot_at, live_at = {}, {}
    for step in range(-2, 3):
        slot, alive = jnp.int32(0), jnp.int32(0)
        for k in range(slots):
            hit = lax.rem((neighbours[0, k] - tile) * side + 2 * tiles - step, tiles) == 0
            slot = jnp.where(hit, k, slot)
            alive = jnp.where(hit, jnp.where(k < live[0], 1, 0), alive)
        slot_at[step], live_at[step] = slot, alive

    def forward(piece, r, step, first=False):
        value = piece[...]
        for n in range(0, width, COLS):
            product = jnp.dot(value, block_v[slot_at[step], :, n:n + COLS], preferred_element_type=F32)
            product = jnp.where(live_at[step] > 0, product, 0.0)
            loc[r, n:n + COLS] = product if first else loc[r, n:n + COLS] + product

    loads[0].wait()
    loads[1].wait()
    for t in range(2):
        for m in range(members):
            pert_f[t, m] = pert_v[t, m].astype(F32)
    for load in loads[4:]:
        load.wait()
    everything = pl.ds(0, members * levels)
    forward(half, everything, 0, first=True)

    def turn(k):
        for n in range(0, width, COLS):
            block_t[k, :, n:n + COLS] = block_v[k, n:n + COLS, :].T

    for copy in ocopies:
        copy.wait_recv()
    forward(precv.at[0], everything, 1)
    loads[2].wait()
    loads[3].wait()

    xcopies, ycopies, passing = {}, {}, {}

    def arrive(c):
        r = rows(c)
        near, far = zcopies[c]
        near.wait_recv()
        passing[c] = start(remote(zrecv.at[0, r], precv.at[1, r], f_s.at[c], f_r.at[c], partner))
        forward(zrecv.at[0, r], r, 2)
        far.wait_recv()
        forward(zrecv.at[1, r], r, -2)

    def contract(c):
        r, lo, size = rows(c), starts[c], CHUNKS[c]
        passing[c].wait_recv()
        forward(precv.at[1, r], r, -1)
        for t in range(2):
            value = jnp.zeros((size, width), F32)
            for m in range(members):
                value = value + pert_f[t, m, lo:lo + size, :] * loc[pl.ds(members * lo + m * size, size)]
            part[t, lo:lo + size, :] = value
        both = part[:, lo:lo + size, :].reshape(2 * size, width)
        mine = pl.ds(2 * lo, 2 * size)
        psend[mine] = both.astype(BF16)
        (along if c in X_FIRST else beyond)(c, psend)

    def along(c, source):
        mine = pl.ds(2 * starts[c], 2 * CHUNKS[c])
        xcopies[c] = [
            start(remote(source.at[mine], xrecv.at[d, mine], m_s.at[d, c], m_r.at[d, c], peers[d]))
            for d in range(len(peers))]

    def beyond(c, source):
        mine = pl.ds(2 * starts[c], 2 * CHUNKS[c])
        ycopies[c] = start(remote(source.at[mine], yrecv.at[mine], g_s.at[c], g_r.at[c], across))

    def with_line(c, summed):
        mine = pl.ds(2 * starts[c], 2 * CHUNKS[c])
        for copy in xcopies[c]:
            copy.wait_recv()
        for d in range(len(peers)):
            summed = summed + xrecv[d, mine].astype(F32)
        return summed

    def with_across(c, summed):
        ycopies[c].wait_recv()
        return summed + yrecv[pl.ds(2 * starts[c], 2 * CHUNKS[c])].astype(F32)

    def merge(c):
        lo, size = starts[c], CHUNKS[c]
        mine = pl.ds(2 * lo, 2 * size)
        summed = part[:, lo:lo + size, :].reshape(2 * size, width)
        summed = (with_line if c in X_FIRST else with_across)(c, summed)
        part[:, lo:lo + size, :] = summed.reshape(2, size, width)
        ysend[mine] = summed.astype(BF16)
        (beyond if c in X_FIRST else along)(c, ysend)

    column = lax.broadcasted_iota(jnp.int32, (1, 1, width), 2)
    observed = column < count[0]
    shares, lones, pairs = {}, {}, {}

    def product(value, step, n):
        out = jnp.dot(value, block_t[slot_at[step], :, n:n + COLS], preferred_element_type=F32)
        return jnp.where(live_at[step] > 0, out, 0.0)

    def adjoint(c):
        r, lo, size = rows(c), starts[c], CHUNKS[c]
        summed = part[:, lo:lo + size, :].reshape(2 * size, width)
        summed = (with_across if c in X_FIRST else with_line)(c, summed).reshape(2, size, width)
        total[:, lo:lo + size, :] = summed
        residual = weight_v[lo:lo + size, :][None] * jnp.where(
            observed, summed - innov_v[:, lo:lo + size, :], 0.0)
        for m in range(0, members, 2):
            two = pert_f[0, m:m + 2, lo:lo + size, :] * residual[0][None]
            two = two + pert_f[1, m:m + 2, lo:lo + size, :] * residual[1][None]
            ain[pl.ds(members * lo + m * size, 2 * size)] = two.reshape(2 * size, width).astype(BF16)
        value = ain[r]
        for n in range(0, width, COLS):
            csend[0, r, n:n + COLS] = product(value, -1, n).astype(BF16)
        shared = start(remote(csend.at[0, r], crecv.at[0, r], c_s.at[0, c], c_r.at[0, c], partner))
        for n in range(0, width, COLS):
            bsend[0, r, n:n + COLS] = product(value, -2, n).astype(BF16)
        lone = start(remote(bsend.at[0, r], brecv.at[0, r], b_s.at[0, c], b_r.at[0, c], behind))
        for n in range(0, width, COLS):
            acc[r, n:n + COLS] = product(value, 2, n)
        shares[c], lones[c] = shared, lone

    def pair(c):
        r = rows(c)
        shares[c].wait_recv()
        bsend[1, r] = (acc[r] + crecv[0, r].astype(F32)).astype(BF16)
        pairs[c] = start(remote(bsend.at[1, r], brecv.at[1, r], b_s.at[1, c], b_r.at[1, c], ahead))

    def rest():
        given = []
        count_half = members * levels // 2
        for part_id in range(2):
            r = pl.ds(part_id * count_half, count_half)
            value = ain[r]
            for n in range(0, width, COLS):
                csend[1, r, n:n + COLS] = product(value, 1, n).astype(BF16)
            given.append(start(remote(csend.at[1, r], crecv.at[1, r], c_s.at[1, part_id], c_r.at[1, part_id], partner)))
        value = ain[...]
        for n in range(0, width, COLS):
            acc[:, n:n + COLS] = product(value, 0, n)
        for copy in given:
            copy.wait_recv()

    def finish(c):
        lo, size = starts[c], CHUNKS[c]
        lones[c].wait_recv()
        pairs[c].wait_recv()
        for m in range(0, members, 2):
            r = pl.ds(members * lo + m * size, 2 * size)
            value = acc[r] + crecv[1, r].astype(F32)
            value = value + coeff_v[m:m + 2, lo:lo + size, :].reshape(2 * size, width)
            value = value + (brecv[0, r].astype(F32) + brecv[1, r].astype(F32))
            grad_out[m:m + 2, lo:lo + size, :] = value.reshape(2, size, width)

    steps = {"z": arrive, "x": contract, "m": merge, "a": adjoint, "b": pair, "t": turn}
    for step in ORDER:
        steps[step[0]](int(step[1:]))
    own = pl.multiple_of(group * (width // groups), width // groups)
    inc_out[...] = total[:, :, pl.ds(own, width // groups)]
    rest()
    for c in range(len(CHUNKS)):
        finish(c)
    for copy in pending:
        copy.wait_send()


def write(inc, grad, inc_out, grad_out, sem):
    members = grad.shape[0]
    copies = [pltpu.make_async_copy(inc, inc_out, sem.at[members])]
    copies += [pltpu.make_async_copy(grad.at[m], grad_out.at[m], sem.at[m]) for m in range(members)]
    for copy in copies:
        copy.start()
    for copy in copies:
        copy.wait()


def shards(coeffs, perturb, blocks, neighbours, live, obs_count, innovation, obs_weight):
    members, levels, width = coeffs.shape
    slots = blocks.shape[1]
    tiles, groups = lax.axis_size("tile"), lax.axis_size("member")
    row_count, chunks, peers = members * levels, len(CHUNKS), groups // 2 - 1
    anywhere = pl.BlockSpec(memory_space=pl.ANY)
    vmem = pl.BlockSpec(memory_space=pltpu.VMEM)
    dma = pltpu.SemaphoreType.DMA
    held = pl.pallas_call(
        functools.partial(kernel, tiles, groups),
        out_shape=(
            pltpu.VMEM((2, levels, width // groups), F32),
            pltpu.VMEM((members, levels, width), F32),
        ),
        in_specs=[anywhere] * 8,
        out_specs=(vmem, vmem),
        scratch_shapes=[
            pltpu.VMEM((members, levels, width), F32),
            pltpu.VMEM((2, members, levels, width), BF16),
            pltpu.VMEM((2, members, levels, width), F32),
            pltpu.VMEM((slots, width, width), BF16),
            pltpu.VMEM((slots, width, width), BF16),
            pltpu.VMEM((2, levels, width), F32),
            pltpu.VMEM((levels, width), F32),
            pltpu.VMEM((row_count, width), BF16),
            pltpu.VMEM((2, row_count, width), BF16),
            pltpu.VMEM((2, row_count, width), BF16),
            pltpu.VMEM((row_count, width), F32),
            pltpu.VMEM((2, levels, width), F32),
            pltpu.VMEM((2 * levels, width), BF16),
            pltpu.VMEM((peers, 2 * levels, width), BF16),
            pltpu.VMEM((2 * levels, width), BF16),
            pltpu.VMEM((2 * levels, width), BF16),
            pltpu.VMEM((2, levels, width), F32),
            pltpu.VMEM((row_count, width), BF16),
            pltpu.VMEM((2, row_count, width), BF16),
            pltpu.VMEM((2, row_count, width), BF16),
            pltpu.VMEM((2, row_count, width), BF16),
            pltpu.VMEM((2, row_count, width), BF16),
            pltpu.VMEM((row_count, width), F32),
            pltpu.SMEM((1, slots), jnp.int32),
            pltpu.SMEM((1,), jnp.int32),
            pltpu.SMEM((1,), jnp.int32),
            dma((3,)),
            dma((members + 4 + slots,)),
            dma((2, chunks)), dma((2, chunks)),
            dma((chunks,)), dma((chunks,)),
            dma((chunks,)), dma((chunks,)),
            dma((peers, chunks)), dma((peers, chunks)),
            dma((chunks,)), dma((chunks,)),
            dma((2, chunks)), dma((2, chunks)),
            dma((2, chunks)), dma((2, chunks)),
        ],
        compiler_params=pltpu.CompilerParams(
            collective_id=0, has_side_effects=True, vmem_limit_bytes=56 * 1024 * 1024),
        cost_estimate=pl.CostEstimate(
            flops=4 * row_count * width * width * slots, bytes_accessed=16 * 1024 * 1024, transcendentals=0),
    )(coeffs, perturb, blocks, neighbours, live, obs_count, innovation, obs_weight)
    held = [pltpu.with_memory_space_constraint(x, pltpu.VMEM) for x in held]
    return pl.pallas_call(
        write,
        out_shape=tuple(jax.ShapeDtypeStruct(x.shape, x.dtype) for x in held),
        in_specs=[anywhere, anywhere],
        out_specs=(anywhere, anywhere),
        scratch_shapes=[dma((members + 1,))],
    )(*held)


def solution(mesh):
    placed = (
        P("member", None, "tile"),
        P(None, "member", None, "tile"),
        P("tile", None, None, None),
        P("tile", None),
        P("tile"),
        P("tile"),
        P(None, None, "tile"),
        P(None, "tile"),
    )
    return jax.shard_map(
        shards,
        mesh=mesh,
        in_specs=placed,
        out_specs=(P(None, None, ("tile", "member")), P("member", None, "tile")),
        check_vma=False,
    )
```

```python
import functools

import jax
import jax.numpy as jnp
from jax import lax
from jax.experimental import pallas as pl
from jax.experimental.pallas import tpu as pltpu
from jax.sharding import PartitionSpec as P

MESH = pl.DeviceIdType.MESH
F32, BF16 = jnp.float32, jnp.bfloat16
CHUNKS = (8, 8, 8, 8)
X_FIRST = (0, 1)
ORDER = (
    "t0", "t1", "z0", "t2", "x0", "z1", "t3", "x1", "z2", "m0", "t4", "x2", "z3", "x3",
    "m1", "a0", "b0", "m2", "m3", "a1", "b1", "a2", "b2", "a3", "b3",
)
COLS = 256


def kernel(tiles, groups, coeffs, perturb, blocks, neighbours_in, live_in, count_in, innovation, weight,
           inc_out, grad_out,
           coeff_v, pert_v, pert_f, block_v, block_t, innov_v, weight_v,
           half, zrecv, precv, loc, part, psend, xrecv, ysend, yrecv, total, ain,
           csend, crecv, bsend, brecv, acc,
           neighbours, live, count, scalar_sem,
           load_sem, z_s, z_r, o_s, o_r, f_s, f_r, m_s, m_r, g_s, g_r, c_s, c_r, b_s, b_r):
    members, levels, width = coeffs.shape
    slots = blocks.shape[1]
    tile, group = lax.axis_index("tile"), lax.axis_index("member")
    side = 1 - 2 * lax.rem(tile, 2)

    def at(step):
        return {"tile": lax.rem(tile + step * side + tiles, tiles)}

    partner, ahead, behind = at(1), at(2), at(-2)
    line = groups // 2
    place = lax.rem(group, line)
    peers = [{"member": group - place + lax.rem(place + d, line)} for d in range(1, line)]
    across = {"member": lax.rem(group + line, groups)}

    def remote(src, dst, send, recv, device):
        return pltpu.make_async_remote_copy(
            src_ref=src, dst_ref=dst, send_sem=send, recv_sem=recv,
            device_id=device, device_id_type=MESH)

    first = [pltpu.make_async_copy(coeffs.at[m], coeff_v.at[m], load_sem.at[4 + slots + m]) for m in range(members)]
    scalars = [
        pltpu.make_async_copy(neighbours_in, neighbours, scalar_sem.at[0]),
        pltpu.make_async_copy(live_in, live, scalar_sem.at[1]),
        pltpu.make_async_copy(count_in, count, scalar_sem.at[2]),
    ]
    loads = [
        pltpu.make_async_copy(perturb.at[0], pert_v.at[0], load_sem.at[0]),
        pltpu.make_async_copy(perturb.at[1], pert_v.at[1], load_sem.at[1]),
        pltpu.make_async_copy(innovation, innov_v, load_sem.at[2]),
        pltpu.make_async_copy(weight, weight_v, load_sem.at[3]),
    ]
    for k in range(slots):
        loads.append(pltpu.make_async_copy(blocks.at[0, k], block_v.at[k], load_sem.at[4 + k]))
    barrier = pltpu.get_barrier_semaphore()
    for device in [ahead, behind, partner, across] + peers:
        pl.semaphore_signal(barrier, inc=1, device_id=device, device_id_type=MESH)
    for load in first + scalars:
        load.start()

    starts = [sum(CHUNKS[:c]) for c in range(len(CHUNKS))]

    def rows(c):
        return pl.ds(members * starts[c], members * CHUNKS[c])

    for load in first:
        load.wait()
    for c, size in enumerate(CHUNKS):
        lo = starts[c]
        for m in range(0, members, 2):
            two = coeff_v[m:m + 2, lo:lo + size, :].reshape(2 * size, width)
            half[pl.ds(members * lo + m * size, 2 * size)] = two.astype(BF16)

    pl.semaphore_wait(barrier, 4 + len(peers))

    pending = []

    def start(copy):
        copy.start()
        pending.append(copy)
        return copy

    zcopies, ocopies = [], []
    for c in range(len(CHUNKS)):
        r = rows(c)
        zcopies.append((
            start(remote(half.at[r], zrecv.at[0, r], z_s.at[0, c], z_r.at[0, c], behind)),
            start(remote(half.at[r], zrecv.at[1, r], z_s.at[1, c], z_r.at[1, c], ahead))))
        if c == 0:
            for load in loads:
                load.start()
        ocopies.append(start(remote(half.at[r], precv.at[0, r], o_s.at[c], o_r.at[c], partner)))

    for load in scalars:
        load.wait()
    slot_at, live_at = {}, {}
    for step in range(-2, 3):
        slot, alive = jnp.int32(0), jnp.int32(0)
        for k in range(slots):
            hit = lax.rem((neighbours[0, k] - tile) * side + 2 * tiles - step, tiles) == 0
            slot = jnp.where(hit, k, slot)
            alive = jnp.where(hit, jnp.where(k < live[0], 1, 0), alive)
        slot_at[step], live_at[step] = slot, alive

    def forward(piece, r, step, first=False):
        value = piece[...]
        for n in range(0, width, COLS):
            product = jnp.dot(value, block_v[slot_at[step], :, n:n + COLS], preferred_element_type=F32)
            product = jnp.where(live_at[step] > 0, product, 0.0)
            loc[r, n:n + COLS] = product if first else loc[r, n:n + COLS] + product

    loads[0].wait()
    loads[1].wait()
    for t in range(2):
        for m in range(members):
            pert_f[t, m] = pert_v[t, m].astype(F32)
    for load in loads[4:]:
        load.wait()
    everything = pl.ds(0, members * levels)
    forward(half, everything, 0, first=True)

    def turn(k):
        for n in range(0, width, COLS):
            block_t[k, :, n:n + COLS] = block_v[k, n:n + COLS, :].T

    for copy in ocopies:
        copy.wait_recv()
    forward(precv.at[0], everything, 1)
    loads[2].wait()
    loads[3].wait()

    xcopies, ycopies, passing = {}, {}, {}

    def arrive(c):
        r = rows(c)
        near, far = zcopies[c]
        near.wait_recv()
        passing[c] = start(remote(zrecv.at[0, r], precv.at[1, r], f_s.at[c], f_r.at[c], partner))
        forward(zrecv.at[0, r], r, 2)
        far.wait_recv()
        forward(zrecv.at[1, r], r, -2)

    def contract(c):
        r, lo, size = rows(c), starts[c], CHUNKS[c]
        passing[c].wait_recv()
        forward(precv.at[1, r], r, -1)
        for t in range(2):
            value = jnp.zeros((size, width), F32)
            for m in range(members):
                value = value + pert_f[t, m, lo:lo + size, :] * loc[pl.ds(members * lo + m * size, size)]
            part[t, lo:lo + size, :] = value
        both = part[:, lo:lo + size, :].reshape(2 * size, width)
        mine = pl.ds(2 * lo, 2 * size)
        psend[mine] = both.astype(BF16)
        (along if c in X_FIRST else beyond)(c, psend)

    def along(c, source):
        mine = pl.ds(2 * starts[c], 2 * CHUNKS[c])
        xcopies[c] = [
            start(remote(source.at[mine], xrecv.at[d, mine], m_s.at[d, c], m_r.at[d, c], peers[d]))
            for d in range(len(peers))]

    def beyond(c, source):
        mine = pl.ds(2 * starts[c], 2 * CHUNKS[c])
        ycopies[c] = start(remote(source.at[mine], yrecv.at[mine], g_s.at[c], g_r.at[c], across))

    def with_line(c, summed):
        mine = pl.ds(2 * starts[c], 2 * CHUNKS[c])
        for copy in xcopies[c]:
            copy.wait_recv()
        for d in range(len(peers)):
            summed = summed + xrecv[d, mine].astype(F32)
        return summed

    def with_across(c, summed):
        ycopies[c].wait_recv()
        return summed + yrecv[pl.ds(2 * starts[c], 2 * CHUNKS[c])].astype(F32)

    def merge(c):
        lo, size = starts[c], CHUNKS[c]
        mine = pl.ds(2 * lo, 2 * size)
        summed = part[:, lo:lo + size, :].reshape(2 * size, width)
        summed = (with_line if c in X_FIRST else with_across)(c, summed)
        part[:, lo:lo + size, :] = summed.reshape(2, size, width)
        ysend[mine] = summed.astype(BF16)
        (beyond if c in X_FIRST else along)(c, ysend)

    column = lax.broadcasted_iota(jnp.int32, (1, 1, width), 2)
    observed = column < count[0]
    shares, lones, pairs = {}, {}, {}

    def product(value, step, n):
        out = jnp.dot(value, block_t[slot_at[step], :, n:n + COLS], preferred_element_type=F32)
        return jnp.where(live_at[step] > 0, out, 0.0)

    def adjoint(c):
        r, lo, size = rows(c), starts[c], CHUNKS[c]
        summed = part[:, lo:lo + size, :].reshape(2 * size, width)
        summed = (with_across if c in X_FIRST else with_line)(c, summed).reshape(2, size, width)
        total[:, lo:lo + size, :] = summed
        residual = weight_v[lo:lo + size, :][None] * jnp.where(
            observed, summed - innov_v[:, lo:lo + size, :], 0.0)
        for m in range(0, members, 2):
            two = pert_f[0, m:m + 2, lo:lo + size, :] * residual[0][None]
            two = two + pert_f[1, m:m + 2, lo:lo + size, :] * residual[1][None]
            ain[pl.ds(members * lo + m * size, 2 * size)] = two.reshape(2 * size, width).astype(BF16)
        value = ain[r]
        for n in range(0, width, COLS):
            csend[0, r, n:n + COLS] = product(value, -1, n).astype(BF16)
        shared = start(remote(csend.at[0, r], crecv.at[0, r], c_s.at[0, c], c_r.at[0, c], partner))
        for n in range(0, width, COLS):
            bsend[0, r, n:n + COLS] = product(value, -2, n).astype(BF16)
        lone = start(remote(bsend.at[0, r], brecv.at[0, r], b_s.at[0, c], b_r.at[0, c], behind))
        for n in range(0, width, COLS):
            acc[r, n:n + COLS] = product(value, 2, n)
        shares[c], lones[c] = shared, lone

    def pair(c):
        r = rows(c)
        shares[c].wait_recv()
        bsend[1, r] = (acc[r] + crecv[0, r].astype(F32)).astype(BF16)
        pairs[c] = start(remote(bsend.at[1, r], brecv.at[1, r], b_s.at[1, c], b_r.at[1, c], ahead))

    def rest():
        given = []
        count_half = members * levels // 2
        for part_id in range(2):
            r = pl.ds(part_id * count_half, count_half)
            value = ain[r]
            for n in range(0, width, COLS):
                csend[1, r, n:n + COLS] = product(value, 1, n).astype(BF16)
            given.append(start(remote(csend.at[1, r], crecv.at[1, r], c_s.at[1, part_id], c_r.at[1, part_id], partner)))
        value = ain[...]
        for n in range(0, width, COLS):
            acc[:, n:n + COLS] = product(value, 0, n)
        for copy in given:
            copy.wait_recv()

    def finish(c):
        lo, size = starts[c], CHUNKS[c]
        lones[c].wait_recv()
        pairs[c].wait_recv()
        for m in range(0, members, 2):
            r = pl.ds(members * lo + m * size, 2 * size)
            value = acc[r] + crecv[1, r].astype(F32)
            value = value + coeff_v[m:m + 2, lo:lo + size, :].reshape(2 * size, width)
            value = value + (brecv[0, r].astype(F32) + brecv[1, r].astype(F32))
            grad_out[m:m + 2, lo:lo + size, :] = value.reshape(2, size, width)

    steps = {"z": arrive, "x": contract, "m": merge, "a": adjoint, "b": pair, "t": turn}
    for step in ORDER:
        steps[step[0]](int(step[1:]))
    own = pl.multiple_of(group * (width // groups), width // groups)
    inc_out[...] = total[:, :, pl.ds(own, width // groups)]
    rest()
    for c in range(len(CHUNKS)):
        finish(c)
    for copy in pending:
        copy.wait_send()


def write(inc, grad, inc_out, grad_out, sem):
    members = grad.shape[0]
    copies = [pltpu.make_async_copy(inc, inc_out, sem.at[members])]
    copies += [pltpu.make_async_copy(grad.at[m], grad_out.at[m], sem.at[m]) for m in range(members)]
    for copy in copies:
        copy.start()
    for copy in copies:
        copy.wait()


def shards(coeffs, perturb, blocks, neighbours, live, obs_count, innovation, obs_weight):
    members, levels, width = coeffs.shape
    slots = blocks.shape[1]
    tiles, groups = lax.axis_size("tile"), lax.axis_size("member")
    row_count, chunks, peers = members * levels, len(CHUNKS), groups // 2 - 1
    anywhere = pl.BlockSpec(memory_space=pl.ANY)
    vmem = pl.BlockSpec(memory_space=pltpu.VMEM)
    dma = pltpu.SemaphoreType.DMA
    held = pl.pallas_call(
        functools.partial(kernel, tiles, groups),
        out_shape=(
            pltpu.VMEM((2, levels, width // groups), F32),
            pltpu.VMEM((members, levels, width), F32),
        ),
        in_specs=[anywhere] * 8,
        out_specs=(vmem, vmem),
        scratch_shapes=[
            pltpu.VMEM((members, levels, width), F32),
            pltpu.VMEM((2, members, levels, width), BF16),
            pltpu.VMEM((2, members, levels, width), F32),
            pltpu.VMEM((slots, width, width), BF16),
            pltpu.VMEM((slots, width, width), BF16),
            pltpu.VMEM((2, levels, width), F32),
            pltpu.VMEM((levels, width), F32),
            pltpu.VMEM((row_count, width), BF16),
            pltpu.VMEM((2, row_count, width), BF16),
            pltpu.VMEM((2, row_count, width), BF16),
            pltpu.VMEM((row_count, width), F32),
            pltpu.VMEM((2, levels, width), F32),
            pltpu.VMEM((2 * levels, width), BF16),
            pltpu.VMEM((peers, 2 * levels, width), BF16),
            pltpu.VMEM((2 * levels, width), BF16),
            pltpu.VMEM((2 * levels, width), BF16),
            pltpu.VMEM((2, levels, width), F32),
            pltpu.VMEM((row_count, width), BF16),
            pltpu.VMEM((2, row_count, width), BF16),
            pltpu.VMEM((2, row_count, width), BF16),
            pltpu.VMEM((2, row_count, width), BF16),
            pltpu.VMEM((2, row_count, width), BF16),
            pltpu.VMEM((row_count, width), F32),
            pltpu.SMEM((1, slots), jnp.int32),
            pltpu.SMEM((1,), jnp.int32),
            pltpu.SMEM((1,), jnp.int32),
            dma((3,)),
            dma((members + 4 + slots,)),
            dma((2, chunks)), dma((2, chunks)),
            dma((chunks,)), dma((chunks,)),
            dma((chunks,)), dma((chunks,)),
            dma((peers, chunks)), dma((peers, chunks)),
            dma((chunks,)), dma((chunks,)),
            dma((2, chunks)), dma((2, chunks)),
            dma((2, chunks)), dma((2, chunks)),
        ],
        compiler_params=pltpu.CompilerParams(
            collective_id=0, has_side_effects=True, vmem_limit_bytes=56 * 1024 * 1024),
        cost_estimate=pl.CostEstimate(
            flops=4 * row_count * width * width * slots, bytes_accessed=16 * 1024 * 1024, transcendentals=0),
    )(coeffs, perturb, blocks, neighbours, live, obs_count, innovation, obs_weight)
    held = [pltpu.with_memory_space_constraint(x, pltpu.VMEM) for x in held]
    return pl.pallas_call(
        write,
        out_shape=tuple(jax.ShapeDtypeStruct(x.shape, x.dtype) for x in held),
        in_specs=[anywhere, anywhere],
        out_specs=(anywhere, anywhere),
        scratch_shapes=[dma((members + 1,))],
    )(*held)


def solution(mesh):
    placed = (
        P("member", None, "tile"),
        P(None, "member", None, "tile"),
        P("tile", None, None, None),
        P("tile", None),
        P("tile"),
        P("tile"),
        P(None, None, "tile"),
        P(None, "tile"),
    )
    return jax.shard_map(
        shards,
        mesh=mesh,
        in_specs=placed,
        out_specs=(P(None, None, ("tile", "member")), P("member", None, "tile")),
        check_vma=False,
    )
```
